32 devices in a mesh: aux: 2 (over y), ao: 16 (over z, x, core).
Axes of the slice: x: 2, y: 2, z: 4, core: 2. Of those that a mesh axis runs over, the one named last changes fastest.
Arguments:
- pair_list: int32 [384, 2], P('ao'), may hold values from 0 to 63, as said below
- pair_count: int32 [16], P('ao'), may hold values from 3 to 24, as said below
- tiles: bfloat16 [384, 8, 128, 128], P('ao', 'aux'), may hold values from -6 to 6
- coeff: bfloat16 [8192, 512], P('ao'), may hold values from -0.25 to 0.25
Outputs:
- k_tiles: bfloat16 [384, 128, 128], P('ao', 'aux')
The draws below stay inside these ranges and needn't reach their ends.
Inputs may be any that keep to these rules, and one draw needn't show every extreme that they name: `pair_list`: each live row of owner o names i among its blocks and i < j < (o + 3) * 4; no live pair repeats; rows past an owner's count repeat that owner's first row. `pair_count`: some owner has exactly 24 live rows.
All inputs are finite; a program needn't handle non-finite values.
Results may differ from the reference program's by a relative error of at most 0.0067.
Values may be sent and summed in bfloat16 or wider, within the bound.
A program may use at most 64 MiB of HBM per device.

```python
import jax
import jax.numpy as jnp
from jax import lax

BLK = 128
OCC = 512
NB_DEV = 4
BAND = 2
PAIR_DEV = 24
AUX = 8
NAO = 8192
PAIRS = 384
N_AO = 16


def pair_plan(key):
    block_total = N_AO * NB_DEV
    window_blocks = (BAND + 1) * NB_DEV
    option_total = NB_DEV * window_blocks
    base_key = jax.random.fold_in(key, 11)
    score_key, shrink_key, fullest_key = jax.random.split(base_key, 3)
    owner_index = jnp.arange(N_AO, dtype=jnp.int32)[:, None]
    option = jnp.arange(option_total, dtype=jnp.int32)[None, :]
    left_pick = option // window_blocks
    right_pick = option % window_blocks
    usable = (right_pick > left_pick) & (owner_index * NB_DEV + right_pick < block_total)
    scores = jax.random.randint(score_key, (N_AO, option_total), 0, 1 << 20) * option_total + option
    scores = scores + jnp.where(usable, 0, 1 << 27).astype(jnp.int32)
    ranking = jnp.argsort(scores, axis=1)[:, :PAIR_DEV].astype(jnp.int32)
    chosen_left = ranking // window_blocks
    chosen_right = ranking % window_blocks
    shrink = jax.random.randint(shrink_key, (N_AO,), 0, 4)
    live_count = jnp.maximum(1, PAIR_DEV // jnp.left_shift(jnp.ones_like(shrink), shrink))
    fullest = jax.random.randint(fullest_key, (), 0, N_AO - BAND)
    live_count = jnp.where(owner_index[:, 0] == fullest, PAIR_DEV, live_count)
    live_count = jnp.minimum(live_count, jnp.sum(usable.astype(jnp.int32), axis=1))
    slot_index = jnp.arange(PAIR_DEV, dtype=jnp.int32)[None, :]
    keep = slot_index < live_count[:, None]
    chosen_left = jnp.where(keep, chosen_left, chosen_left[:, :1])
    chosen_right = jnp.where(keep, chosen_right, chosen_right[:, :1])
    left_block = owner_index * NB_DEV + chosen_left
    right_block = owner_index * NB_DEV + chosen_right
    pair_rows = jnp.stack([left_block, right_block], -1).reshape(N_AO * PAIR_DEV, 2).astype(jnp.int32)
    return (pair_rows, live_count.astype(jnp.int32))


def draw_pair_list(key, part):
    pair_rows, live_count = pair_plan(key)
    return pair_rows


def draw_pair_count(key, part):
    pair_rows, live_count = pair_plan(key)
    return live_count


def shard_levels(stream_key, shape, cuts, least, top_value):
    def one(dim, parts):
        steps = jax.random.uniform(jax.random.fold_in(jax.random.fold_in(stream_key, 6), dim), (parts,), jnp.float32, least / len(cuts), top_value / len(cuts))
        return jnp.repeat(jnp.exp(steps), shape[dim] // parts).reshape((-1,) + (1,) * (len(shape) - dim - 1))

    gain = one(*cuts[0])
    for cut in cuts[1:]:
        gain = gain * one(*cut)
    return gain


def noise(stream_key, dims, deviation, limit, cuts=(), kind=jnp.bfloat16):
    factor_of = shard_levels(stream_key, dims, cuts, -0.22, 0.18) if cuts else 1.0
    drawn = jax.random.normal(stream_key, dims, jnp.float32) * deviation * factor_of
    return jnp.minimum(jnp.maximum(drawn, -limit), limit).astype(kind)


def setup_inputs(seed: int = 0) -> dict:
    key_list = jax.random.split(jax.random.key(seed), 5)
    pair_list = draw_pair_list(jax.random.fold_in(key_list[4], 71), 0)
    pair_count = draw_pair_count(jax.random.fold_in(key_list[4], 71), 0)
    tiles = noise(key_list[2], (PAIRS, AUX, BLK, BLK), 1.0, 6.0, ((0, 16), (1, 2)))
    coeff = noise(key_list[3], (NAO, OCC), (BLK * 5) ** -0.5, 0.25, ((0, 16),))
    return dict(pair_list=pair_list, pair_count=pair_count, tiles=tiles, coeff=coeff)


def reference(pair_list, pair_count, tiles, coeff):
    block_total = N_AO * NB_DEV
    window_blocks = (BAND + 1) * NB_DEV
    blocks = coeff.reshape(block_total, BLK, OCC)
    padded = jnp.concatenate([blocks, jnp.zeros((BAND * NB_DEV, BLK, OCC), blocks.dtype)], 0)
    pair_rows = pair_list.reshape(N_AO, PAIR_DEV, 2)
    grouped = tiles.reshape(N_AO, PAIR_DEV, AUX, BLK, BLK)

    def owner_step(running, inputs):
        owner_index, owner_pairs, live_count, owner_tiles = inputs
        first_block = owner_index * NB_DEV
        window = lax.dynamic_slice_in_dim(padded, first_block, window_blocks, 0).astype(jnp.float32)

        def add_pair(slot_index, totals):
            left_block = (owner_pairs[slot_index, 0] - first_block).astype(jnp.int32)
            right_block = (owner_pairs[slot_index, 1] - first_block).astype(jnp.int32)
            is_live = slot_index < live_count
            pair_tile = owner_tiles[slot_index].astype(jnp.float32)
            to_left = jnp.einsum("pmn,nk->pmk", pair_tile, window[right_block])
            to_right = jnp.einsum("pmn,mk->pnk", pair_tile, window[left_block])
            nothing = jnp.zeros_like(to_left)
            totals = totals.at[left_block].add(jnp.where(is_live, to_left, nothing))
            return totals.at[right_block].add(jnp.where(is_live, to_right, nothing))

        totals = lax.fori_loop(0, PAIR_DEV, add_pair, jnp.zeros((window_blocks, AUX, BLK, OCC), jnp.float32))
        halves = lax.optimization_barrier(totals.astype(jnp.bfloat16)).astype(jnp.float32)
        running = running + halves
        finished = running[:NB_DEV].astype(jnp.bfloat16)
        running = jnp.concatenate([running[NB_DEV:], jnp.zeros((NB_DEV, AUX, BLK, OCC), jnp.float32)], 0)
        return running, finished

    owners = jnp.arange(N_AO, dtype=jnp.int32)
    start = jnp.zeros((window_blocks, AUX, BLK, OCC), jnp.float32)
    _, fitted = lax.scan(owner_step, start, (owners, pair_rows, pair_count, grouped))
    fitted = fitted.reshape(block_total, AUX, BLK, OCC)
    norm_factor = (AUX * OCC) ** -0.5
    slot_ids = jnp.arange(N_AO * PAIR_DEV, dtype=jnp.int32)
    flat_live = (slot_ids % PAIR_DEV) < jnp.repeat(pair_count, PAIR_DEV)

    def contract(entry_pair):
        pair_row, is_live = entry_pair
        left_rows = fitted[pair_row[0]].astype(jnp.float32)
        right_rows = fitted[pair_row[1]].astype(jnp.float32)
        pair_tile = jnp.einsum("pmk,pnk->mn", left_rows, right_rows) * norm_factor
        return jnp.where(is_live, pair_tile, jnp.zeros_like(pair_tile)).astype(jnp.bfloat16)

    return lax.map(contract, (pair_list, flat_live))
```

```python
import functools

import jax
import jax.numpy as jnp
from jax import lax
from jax.experimental import pallas as pl
from jax.experimental.pallas import tpu as pltpu
from jax.sharding import PartitionSpec as P

GROUP = 4
REACH = 2
VMEM_LIMIT = 48 * 1024 * 1024


def swapped(value, count, bit):
    return lax.ppermute(value, "ao", [(k, k ^ bit) for k in range(count)])


def shifted(value, count, steps):
    lo, hi = max(0, -steps), min(count, count - steps)
    return lax.ppermute(value, "ao", [(k, k + steps) for k in range(lo, hi)])


def halves_kernel(blocks, info, pairs, *refs):
    tiles = refs[:GROUP]
    own, across, core_pair, ahead_a, ahead_b = refs[GROUP : GROUP + 5]
    keep_ref, send_ref = refs[GROUP + 5 : GROUP + 7]
    tile_v, coeff_v, totals, sems = refs[GROUP + 7 :]
    me = info[0]
    first = info[1]

    def place(source, start, index):
        return pltpu.make_async_copy(
            source, coeff_v.at[pl.ds(start * blocks, blocks)], sems.at[index]
        )

    copies = [
        place(own, me, 0),
        place(across, me ^ 2, 1),
        place(core_pair.at[0], me ^ 1, 2),
        place(core_pair.at[1], me ^ 3, 3),
        place(ahead_a, GROUP + (me & 1), 4),
        place(ahead_b, GROUP + 1 - (me & 1), 5),
    ]
    copies += [
        pltpu.make_async_copy(tiles[d], tile_v.at[d], sems.at[6 + d]) for d in range(GROUP)
    ]
    for copy in copies:
        copy.start()
    totals[...] = jnp.zeros_like(totals)
    for copy in copies:
        copy.wait()

    aux_local = tile_v.shape[2]
    for d in range(GROUP):

        def step(slot, carry):
            left = pairs[d, 2 * slot] - first
            right = pairs[d, 2 * slot + 1] - first
            for aux in range(aux_local):
                tile = tile_v[d, slot, aux]
                totals[left, aux] += lax.dot_general(
                    tile, coeff_v[right], (((1,), (0,)), ((), ())),
                    preferred_element_type=jnp.float32,
                )
                totals[right, aux] += lax.dot_general(
                    tile, coeff_v[left], (((0,), (0,)), ((), ())),
                    preferred_element_type=jnp.float32,
                )
            return carry

        lax.fori_loop(0, info[2 + d], step, 0)

    inside = GROUP * blocks
    keep_ref[...] = totals[:inside]
    send_ref[...] = totals[inside:].astype(send_ref.dtype)


def contract_kernel(blocks, info, pairs, own, ahead, keep_ref, send_ref, window, sems):
    first = info[1]
    inside = GROUP * blocks
    copies = [
        pltpu.make_async_copy(own, window.at[pl.ds(0, inside)], sems.at[0]),
        pltpu.make_async_copy(ahead, window.at[pl.ds(inside, REACH * blocks)], sems.at[1]),
    ]
    for copy in copies:
        copy.start()
    for copy in copies:
        copy.wait()
    aux_local = window.shape[1]
    for d in range(GROUP):
        target = (keep_ref, send_ref)[d & 1]

        def step(slot, carry):
            left = pairs[d, 2 * slot] - first
            right = pairs[d, 2 * slot + 1] - first
            total = None
            for aux in range(aux_local):
                part = lax.dot_general(
                    window[left, aux], window[right, aux], (((1,), (1,)), ((), ())),
                    preferred_element_type=jnp.float32,
                )
                total = part if total is None else total + part
            target[d >> 1, slot] = total.astype(target.dtype)
            return carry

        def blank(slot, carry):
            target[d >> 1, slot] = jnp.zeros(target.shape[2:], target.dtype)
            return carry

        lax.fori_loop(0, info[2 + d], step, 0)
        lax.fori_loop(info[2 + d], target.shape[1], blank, 0)


def on_device(pair_list, pair_count, tiles, coeff):
    slots, aux_all, size, _ = tiles.shape
    orbitals = coeff.shape[1]
    blocks = coeff.shape[0] // size
    owners = lax.axis_size("ao")
    aux_parts = lax.axis_size("aux")
    aux_local = aux_all // GROUP
    owner = lax.axis_index("ao")
    me = owner % GROUP
    first = (owner - me) * blocks
    swap = functools.partial(swapped, count=owners)

    own = coeff.reshape(blocks, size, orbitals)
    across = swap(own, bit=2)
    core_pair = swap(jnp.stack([own, across]), bit=1)
    ahead_a = shifted(jnp.where(me < REACH, own, across), owners, -GROUP)
    ahead_b = swap(ahead_a, bit=1)

    listed = jnp.concatenate([pair_list.reshape(-1), pair_count]).reshape(1, -1)
    lists = jnp.concatenate([listed] + [swap(listed, bit=d) for d in range(1, GROUP)], 0)
    counts = lists[:, 2 * slots]
    info = jnp.concatenate([jnp.stack([me, first]).astype(jnp.int32), counts])

    def part_of(member):
        return lax.dynamic_slice_in_dim(tiles, member * aux_local, aux_local, 1)

    group_tiles = [part_of(me)] + [
        swap(part_of(me ^ d), bit=d) for d in range(1, GROUP)
    ]

    smem = pl.BlockSpec(memory_space=pltpu.SMEM)
    anywhere = pl.BlockSpec(memory_space=pl.ANY)
    vmem = pl.BlockSpec(memory_space=pltpu.VMEM)
    inside, outside = GROUP * blocks, REACH * blocks
    window = inside + outside
    keep, send = pl.pallas_call(
        functools.partial(halves_kernel, blocks),
        out_shape=(
            jax.ShapeDtypeStruct((inside, aux_local, size, orbitals), jnp.float32),
            jax.ShapeDtypeStruct((outside, aux_local, size, orbitals), jnp.bfloat16),
        ),
        in_specs=[smem] * 2 + [anywhere] * (GROUP + 5),
        out_specs=(vmem, vmem),
        scratch_shapes=[
            pltpu.VMEM((GROUP, slots, aux_local, size, size), jnp.bfloat16),
            pltpu.VMEM((window, size, orbitals), jnp.bfloat16),
            pltpu.VMEM((window, aux_local, size, orbitals), jnp.float32),
            pltpu.SemaphoreType.DMA((6 + GROUP,)),
        ],
        compiler_params=pltpu.CompilerParams(vmem_limit_bytes=VMEM_LIMIT),
        name="halves",
    )(info, lists, *group_tiles, own, across, core_pair, ahead_a, ahead_b)

    arrived = shifted(send, owners, GROUP)
    near = (keep[:outside] + arrived.astype(jnp.float32)).astype(jnp.bfloat16)
    fitted = jnp.concatenate([near, keep[outside:].astype(jnp.bfloat16)], 0)
    fitted_ahead = shifted(near, owners, -GROUP)

    kept, sent = pl.pallas_call(
        functools.partial(contract_kernel, blocks),
        out_shape=(
            jax.ShapeDtypeStruct((2, slots, size, size), jnp.float32),
            jax.ShapeDtypeStruct((2, slots, size, size), jnp.bfloat16),
        ),
        in_specs=[smem] * 2 + [anywhere] * 2,
        out_specs=(vmem, vmem),
        scratch_shapes=[
            pltpu.VMEM((window, aux_local, size, orbitals), jnp.bfloat16),
            pltpu.SemaphoreType.DMA((2,)),
        ],
        compiler_params=pltpu.CompilerParams(vmem_limit_bytes=VMEM_LIMIT),
        name="contract",
    )(info, lists, fitted, fitted_ahead)

    both = kept + swap(sent, bit=1).astype(jnp.float32)
    mine = both[0] + swap(both[1].astype(jnp.bfloat16), bit=2).astype(jnp.float32)
    norm_factor = (aux_all * aux_parts * orbitals) ** (-0.5)
    if aux_parts == 2:
        rows = size // 2
        side = lax.axis_index("aux")
        away = lax.dynamic_slice_in_dim(mine, (1 - side) * rows, rows, 1)
        here = lax.dynamic_slice_in_dim(mine, side * rows, rows, 1)
        other = lax.ppermute(away.astype(jnp.bfloat16), "aux", [(0, 1), (1, 0)])
        summed = here + other.astype(jnp.float32)
    else:
        summed = lax.psum_scatter(mine, "aux", scatter_dimension=1, tiled=True)
    return (summed * norm_factor).astype(jnp.bfloat16)


def solution(mesh):
    in_specs = (P("ao", None), P("ao"), P("ao", "aux", None, None), P("ao", None))
    out_specs = P("ao", "aux", None)
    return jax.shard_map(
        on_device, mesh=mesh, in_specs=in_specs, out_specs=out_specs, check_vma=False
    )
```

```python
import functools

import jax
import jax.numpy as jnp
from jax import lax
from jax.experimental import pallas as pl
from jax.experimental.pallas import tpu as pltpu
from jax.sharding import PartitionSpec as P

GROUP = 4
REACH = 2
CHUNKS = 2
UNROLL = 4
VMEM_LIMIT = 48 * 1024 * 1024


def swapped(value, count, bit):
    return lax.ppermute(value, "ao", [(k, k ^ bit) for k in range(count)])


def shifted(value, count, steps):
    lo, hi = max(0, -steps), min(count, count - steps)
    return lax.ppermute(value, "ao", [(k, k + steps) for k in range(lo, hi)])


def halves_kernel(blocks, columns, info, pairs, *refs):
    tiles = refs[:GROUP]
    own, across, core_pair, ahead_a, ahead_b = refs[GROUP : GROUP + 5]
    keep_ref, send_ref = refs[GROUP + 5 : GROUP + 7]
    tile_v, coeff_v, totals, sems = refs[GROUP + 7 :]
    me = info[0]
    first = info[1]

    def place(source, start, index):
        return pltpu.make_async_copy(
            source.at[:, :, columns],
            coeff_v.at[pl.ds(start * blocks, blocks)],
            sems.at[index],
        )

    copies = [
        place(own, me, 0),
        place(across, me ^ 2, 1),
        place(core_pair.at[0], me ^ 1, 2),
        place(core_pair.at[1], me ^ 3, 3),
        place(ahead_a, GROUP + (me & 1), 4),
        place(ahead_b, GROUP + 1 - (me & 1), 5),
    ]
    copies += [
        pltpu.make_async_copy(tiles[d], tile_v.at[d], sems.at[6 + d]) for d in range(GROUP)
    ]
    for copy in copies:
        copy.start()
    totals[...] = jnp.zeros_like(totals)
    for copy in copies:
        copy.wait()

    aux_local = tile_v.shape[2]
    for d in range(GROUP):
        count = info[2 + d]

        def step(turn, carry):
            for aux in range(aux_local):
                updates = []
                for k in range(UNROLL):
                    slot = turn * UNROLL + k
                    left = pairs[d, 2 * slot] - first
                    right = pairs[d, 2 * slot + 1] - first
                    tile = tile_v[d, slot, aux]
                    tile = jnp.where(slot < count, tile, jnp.zeros_like(tile))
                    to_left = lax.dot_general(
                        tile, coeff_v[right], (((1,), (0,)), ((), ())),
                        preferred_element_type=jnp.float32,
                    )
                    to_right = lax.dot_general(
                        tile, coeff_v[left], (((0,), (0,)), ((), ())),
                        preferred_element_type=jnp.float32,
                    )
                    updates += [(left, to_left), (right, to_right)]
                for block, update in updates:
                    totals[block, aux] += update
            return carry

        lax.fori_loop(0, (count + UNROLL - 1) // UNROLL, step, 0)

    inside = GROUP * blocks
    keep_ref[...] = totals[:inside]
    send_ref[...] = totals[inside:].astype(send_ref.dtype)


def contract_kernel(blocks, earlier, info, pairs, *refs):
    own, ahead = refs[:2]
    before = refs[2:4] if earlier else None
    keep_ref, send_ref, window, sems = refs[-4:]
    first = info[1]
    inside = GROUP * blocks
    copies = [
        pltpu.make_async_copy(own, window.at[pl.ds(0, inside)], sems.at[0]),
        pltpu.make_async_copy(ahead, window.at[pl.ds(inside, REACH * blocks)], sems.at[1]),
    ]
    for copy in copies:
        copy.start()
    for copy in copies:
        copy.wait()
    aux_local = window.shape[1]
    for d in range(GROUP):
        target = (keep_ref, send_ref)[d & 1]
        base = before[d & 1] if earlier else None
        count = info[2 + d]

        def step(turn, carry):
            results = []
            for k in range(UNROLL):
                slot = turn * UNROLL + k
                left = pairs[d, 2 * slot] - first
                right = pairs[d, 2 * slot + 1] - first
                total = base[d >> 1, slot] if earlier else None
                for aux in range(aux_local):
                    part = lax.dot_general(
                        window[left, aux], window[right, aux], (((1,), (1,)), ((), ())),
                        preferred_element_type=jnp.float32,
                    )
                    total = part if total is None else total + part
                total = jnp.where(slot < count, total, jnp.zeros_like(total))
                results.append((slot, total))
            for slot, total in results:
                target[d >> 1, slot] = total.astype(target.dtype)
            return carry

        def blank(turn, carry):
            for k in range(UNROLL):
                target[d >> 1, turn * UNROLL + k] = jnp.zeros(target.shape[2:], target.dtype)
            return carry

        turns = (count + UNROLL - 1) // UNROLL
        lax.fori_loop(0, turns, step, 0)
        lax.fori_loop(turns, target.shape[1] // UNROLL, blank, 0)


def on_device(pair_list, pair_count, tiles, coeff):
    slots, aux_all, size, _ = tiles.shape
    orbitals = coeff.shape[1]
    blocks = coeff.shape[0] // size
    owners = lax.axis_size("ao")
    aux_parts = lax.axis_size("aux")
    aux_local = aux_all // GROUP
    owner = lax.axis_index("ao")
    me = owner % GROUP
    first = (owner - me) * blocks
    swap = functools.partial(swapped, count=owners)

    def part_of(member):
        return lax.dynamic_slice_in_dim(tiles, member * aux_local, aux_local, 1)

    own = coeff.reshape(blocks, size, orbitals)
    parts, own = lax.optimization_barrier(([part_of(me ^ d) for d in range(GROUP)], own))
    group_tiles = parts[:1] + [swap(parts[d], bit=d) for d in range(1, GROUP)]
    across, group_tiles[2] = lax.optimization_barrier((swap(own, bit=2), group_tiles[2]))
    core_pair = swap(jnp.stack([own, across]), bit=1)
    ahead_a = shifted(jnp.where(me < REACH, own, across), owners, -GROUP)
    ahead_b = swap(ahead_a, bit=1)

    listed = jnp.concatenate([pair_list.reshape(-1), pair_count]).reshape(1, -1)
    lists = jnp.concatenate([listed] + [swap(listed, bit=d) for d in range(1, GROUP)], 0)
    counts = lists[:, 2 * slots]
    info = jnp.concatenate([jnp.stack([me, first]).astype(jnp.int32), counts])

    smem = pl.BlockSpec(memory_space=pltpu.SMEM)
    anywhere = pl.BlockSpec(memory_space=pl.ANY)
    vmem = pl.BlockSpec(memory_space=pltpu.VMEM)
    inside, outside = GROUP * blocks, REACH * blocks
    window = inside + outside
    width = orbitals // CHUNKS

    def halves(chunk):
        columns = slice(chunk * width, (chunk + 1) * width)
        return pl.pallas_call(
            functools.partial(halves_kernel, blocks, columns),
            out_shape=(
                jax.ShapeDtypeStruct((inside, aux_local, size, width), jnp.float32),
                jax.ShapeDtypeStruct((outside, aux_local, size, width), jnp.bfloat16),
            ),
            in_specs=[smem] * 2 + [anywhere] * (GROUP + 5),
            out_specs=(vmem, vmem),
            scratch_shapes=[
                pltpu.VMEM((GROUP, slots, aux_local, size, size), jnp.bfloat16),
                pltpu.VMEM((window, size, width), jnp.bfloat16),
                pltpu.VMEM((window, aux_local, size, width), jnp.float32),
                pltpu.SemaphoreType.DMA((6 + GROUP,)),
            ],
            compiler_params=pltpu.CompilerParams(vmem_limit_bytes=VMEM_LIMIT),
            cost_estimate=pl.CostEstimate(
                flops=8 * GROUP * slots * aux_local * size * size * width,
                bytes_accessed=32 * 1024 * 1024,
                transcendentals=0,
            ),
            name="halves",
        )(info, lists, *group_tiles, own, across, core_pair, ahead_a, ahead_b)

    def contract(fitted, fitted_ahead, before):
        last = len(before) > 0
        return pl.pallas_call(
            functools.partial(contract_kernel, blocks, last),
            out_shape=(
                jax.ShapeDtypeStruct((2, slots, size, size), jnp.float32),
                jax.ShapeDtypeStruct(
                    (2, slots, size, size), jnp.bfloat16 if last else jnp.float32
                ),
            ),
            in_specs=[smem] * 2 + [anywhere] * 2 + [vmem] * len(before),
            out_specs=(vmem, vmem),
            scratch_shapes=[
                pltpu.VMEM((window, aux_local, size, width), jnp.bfloat16),
                pltpu.SemaphoreType.DMA((2,)),
            ],
            compiler_params=pltpu.CompilerParams(vmem_limit_bytes=VMEM_LIMIT),
            cost_estimate=pl.CostEstimate(
                flops=4 * GROUP * slots * aux_local * size * size * width,
                bytes_accessed=32 * 1024 * 1024,
                transcendentals=0,
            ),
            name="contract",
        )(info, lists, fitted, fitted_ahead, *before)

    keep0, send0 = halves(0)
    arrived0 = shifted(send0, owners, GROUP)
    keep1, send1 = halves(1)
    arrived0, keep1, send1 = lax.optimization_barrier((arrived0, keep1, send1))

    def finish(keep, arrived):
        near = (keep[:outside] + arrived.astype(jnp.float32)).astype(jnp.bfloat16)
        return near, jnp.concatenate([near, keep[outside:].astype(jnp.bfloat16)], 0)

    arrived1 = shifted(send1, owners, GROUP)
    near0, fitted0 = finish(keep0, arrived0)
    ahead0 = shifted(near0, owners, -GROUP)
    near1, fitted1 = finish(keep1, arrived1)
    ahead0, near1, fitted1 = lax.optimization_barrier((ahead0, near1, fitted1))
    ahead1 = shifted(near1, owners, -GROUP)
    before = contract(fitted0, ahead0, ())
    kept, sent = contract(fitted1, ahead1, before)

    norm_factor = (aux_all * aux_parts * orbitals) ** (-0.5)
    both = kept + swap(sent, bit=1).astype(jnp.float32)

    def through_pair(value):
        return value[0] + swap(value[1].astype(jnp.bfloat16), bit=2).astype(jnp.float32)

    if aux_parts == 2:
        rows = size // 2
        side = lax.axis_index("aux")

        def through_aux(value):
            dim = value.ndim - 2
            away = lax.dynamic_slice_in_dim(value, (1 - side) * rows, rows, dim)
            here = lax.dynamic_slice_in_dim(value, side * rows, rows, dim)
            other = lax.ppermute(away.astype(jnp.bfloat16), "aux", [(0, 1), (1, 0)])
            return here + other.astype(jnp.float32)

        cut = slots // 2
        early = through_aux(through_pair(both[:, :cut]))
        late = through_pair(through_aux(both[:, cut:]))
        summed = jnp.concatenate([early, late], 0)
    else:
        summed = lax.psum_scatter(through_pair(both), "aux", scatter_dimension=1, tiled=True)
    return (summed * norm_factor).astype(jnp.bfloat16)


def solution(mesh):
    in_specs = (P("ao", None), P("ao"), P("ao", "aux", None, None), P("ao", None))
    out_specs = P("ao", "aux", None)
    return jax.shard_map(
        on_device, mesh=mesh, in_specs=in_specs, out_specs=out_specs, check_vma=False
    )
```

```python
import functools

import jax
import jax.numpy as jnp
from jax import lax
from jax.experimental import pallas as pl
from jax.experimental.pallas import tpu as pltpu
from jax.sharding import PartitionSpec as P

GROUP = 4
REACH = 2
CHUNKS = 2
UNROLL = 4
VMEM_LIMIT = 48 * 1024 * 1024


def swapped(value, count, bit):
    return lax.ppermute(value, "ao", [(k, k ^ bit) for k in range(count)])


def shifted(value, count, steps):
    lo, hi = max(0, -steps), min(count, count - steps)
    return lax.ppermute(value, "ao", [(k, k + steps) for k in range(lo, hi)])


def halves_kernel(blocks, columns, info, pairs, *refs):
    tiles = refs[:GROUP]
    own, across, core_pair, ahead_a, ahead_b = refs[GROUP : GROUP + 5]
    keep_ref, send_ref = refs[GROUP + 5 : GROUP + 7]
    tile_v, coeff_v, totals, sems = refs[GROUP + 7 :]
    me = info[0]
    first = info[1]

    def place(source, start, index):
        return pltpu.make_async_copy(
            source.at[:, :, columns],
            coeff_v.at[pl.ds(start * blocks, blocks)],
            sems.at[index],
        )

    copies = [
        place(own, me, 0),
        place(across, me ^ 2, 1),
        place(core_pair.at[0], me ^ 1, 2),
        place(core_pair.at[1], me ^ 3, 3),
        place(ahead_a, GROUP + (me & 1), 4),
        place(ahead_b, GROUP + 1 - (me & 1), 5),
    ]
    copies += [
        pltpu.make_async_copy(tiles[d], tile_v.at[d], sems.at[6 + d]) for d in range(GROUP)
    ]
    for copy in copies:
        copy.start()
    totals[...] = jnp.zeros_like(totals)
    for copy in copies:
        copy.wait()

    aux_local = tile_v.shape[2]
    for d in range(GROUP):
        count = info[2 + d]

        def step(turn, carry):
            for aux in range(aux_local):
                updates = []
                for k in range(UNROLL):
                    slot = turn * UNROLL + k
                    left = pairs[d, 2 * slot] - first
                    right = pairs[d, 2 * slot + 1] - first
                    tile = tile_v[d, slot, aux]
                    tile = jnp.where(slot < count, tile, jnp.zeros_like(tile))
                    to_left = lax.dot_general(
                        tile, coeff_v[right], (((1,), (0,)), ((), ())),
                        preferred_element_type=jnp.float32,
                    )
                    to_right = lax.dot_general(
                        tile, coeff_v[left], (((0,), (0,)), ((), ())),
                        preferred_element_type=jnp.float32,
                    )
                    updates += [(left, to_left), (right, to_right)]
                for block, update in updates:
                    totals[block, aux] += update
            return carry

        lax.fori_loop(0, (count + UNROLL - 1) // UNROLL, step, 0)

    inside = GROUP * blocks
    keep_ref[...] = totals[:inside]
    send_ref[...] = totals[inside:].astype(send_ref.dtype)


def contract_kernel(blocks, ranges, earlier, info, pairs, *refs):
    own, ahead = refs[:2]
    before = refs[2:4] if earlier else None
    window, sems = refs[-2:]
    outs = refs[-2 - 2 * len(ranges) : -2]
    first = info[1]
    inside = GROUP * blocks
    copies = [
        pltpu.make_async_copy(own, window.at[pl.ds(0, inside)], sems.at[0]),
        pltpu.make_async_copy(ahead, window.at[pl.ds(inside, REACH * blocks)], sems.at[1]),
    ]
    for copy in copies:
        copy.start()
    for copy in copies:
        copy.wait()
    aux_local = window.shape[1]
    for r, (start, length) in enumerate(ranges):
        for d in range(GROUP):
            target = outs[2 * r + (d & 1)]
            base = before[d & 1] if earlier else None
            count = jnp.clip(info[2 + d] - start, 0, length)

            def step(turn, carry):
                results = []
                for k in range(UNROLL):
                    slot = turn * UNROLL + k
                    left = pairs[d, 2 * (start + slot)] - first
                    right = pairs[d, 2 * (start + slot) + 1] - first
                    total = base[d >> 1, slot] if earlier else None
                    for aux in range(aux_local):
                        part = lax.dot_general(
                            window[left, aux], window[right, aux], (((1,), (1,)), ((), ())),
                            preferred_element_type=jnp.float32,
                        )
                        total = part if total is None else total + part
                    total = jnp.where(slot < count, total, jnp.zeros_like(total))
                    results.append((slot, total))
                for slot, total in results:
                    target[d >> 1, slot] = total.astype(target.dtype)
                return carry

            def blank(turn, carry):
                for k in range(UNROLL):
                    target[d >> 1, turn * UNROLL + k] = jnp.zeros(target.shape[2:], target.dtype)
                return carry

            turns = (count + UNROLL - 1) // UNROLL
            lax.fori_loop(0, turns, step, 0)
            lax.fori_loop(turns, length // UNROLL, blank, 0)


def on_device(pair_list, pair_count, tiles, coeff):
    slots, aux_all, size, _ = tiles.shape
    orbitals = coeff.shape[1]
    blocks = coeff.shape[0] // size
    owners = lax.axis_size("ao")
    aux_parts = lax.axis_size("aux")
    aux_local = aux_all // GROUP
    owner = lax.axis_index("ao")
    me = owner % GROUP
    first = (owner - me) * blocks
    swap = functools.partial(swapped, count=owners)

    def part_of(member):
        return lax.dynamic_slice_in_dim(tiles, member * aux_local, aux_local, 1)

    own = coeff.reshape(blocks, size, orbitals)
    near_part = swap(part_of(me ^ 1), bit=1)
    crossing = swap(jnp.stack([part_of(me ^ 2), part_of(me ^ 3)]), bit=2)
    group_tiles = [part_of(me), near_part, crossing[0], swap(crossing[1], bit=1)]
    listed = jnp.concatenate([pair_list.reshape(-1), pair_count]).reshape(1, -1)
    lists = jnp.concatenate([listed] + [swap(listed, bit=d) for d in range(1, GROUP)], 0)
    across, lists = lax.optimization_barrier((swap(own, bit=2), lists))
    core_pair = swap(jnp.stack([own, across]), bit=1)
    ahead_a = shifted(jnp.where(me < REACH, own, across), owners, -GROUP)
    ahead_b = swap(ahead_a, bit=1)

    counts = lists[:, 2 * slots]
    info = jnp.concatenate([jnp.stack([me, first]).astype(jnp.int32), counts])

    smem = pl.BlockSpec(memory_space=pltpu.SMEM)
    anywhere = pl.BlockSpec(memory_space=pl.ANY)
    vmem = pl.BlockSpec(memory_space=pltpu.VMEM)
    inside, outside = GROUP * blocks, REACH * blocks
    window = inside + outside
    width = orbitals // CHUNKS

    def halves(chunk):
        columns = slice(chunk * width, (chunk + 1) * width)
        return pl.pallas_call(
            functools.partial(halves_kernel, blocks, columns),
            out_shape=(
                jax.ShapeDtypeStruct((inside, aux_local, size, width), jnp.float32),
                jax.ShapeDtypeStruct((outside, aux_local, size, width), jnp.bfloat16),
            ),
            in_specs=[smem] * 2 + [anywhere] * (GROUP + 5),
            out_specs=(vmem, vmem),
            scratch_shapes=[
                pltpu.VMEM((GROUP, slots, aux_local, size, size), jnp.bfloat16),
                pltpu.VMEM((window, size, width), jnp.bfloat16),
                pltpu.VMEM((window, aux_local, size, width), jnp.float32),
                pltpu.SemaphoreType.DMA((6 + GROUP,)),
            ],
            compiler_params=pltpu.CompilerParams(vmem_limit_bytes=VMEM_LIMIT),
            cost_estimate=pl.CostEstimate(
                flops=8 * GROUP * slots * aux_local * size * size * width,
                bytes_accessed=32 * 1024 * 1024,
                transcendentals=0,
            ),
            name="halves",
        )(info, lists, *group_tiles, own, across, core_pair, ahead_a, ahead_b)

    def contract(fitted, fitted_ahead, ranges, before):
        last = len(before) > 0
        shapes = []
        for _, length in ranges:
            shape = (2, length, size, size)
            shapes.append(jax.ShapeDtypeStruct(shape, jnp.float32))
            shapes.append(jax.ShapeDtypeStruct(shape, jnp.bfloat16 if last else jnp.float32))
        return pl.pallas_call(
            functools.partial(contract_kernel, blocks, ranges, last),
            out_shape=tuple(shapes),
            in_specs=[smem] * 2 + [anywhere] * 2 + [vmem] * len(before),
            out_specs=(vmem,) * len(shapes),
            scratch_shapes=[
                pltpu.VMEM((window, aux_local, size, width), jnp.bfloat16),
                pltpu.SemaphoreType.DMA((2,)),
            ],
            compiler_params=pltpu.CompilerParams(vmem_limit_bytes=VMEM_LIMIT),
            cost_estimate=pl.CostEstimate(
                flops=4 * GROUP * slots * aux_local * size * size * width,
                bytes_accessed=16 * 1024 * 1024,
                transcendentals=0,
            ),
            name="contract",
        )(info, lists, fitted, fitted_ahead, *before)

    keep0, send0 = halves(0)
    arrived0 = shifted(send0, owners, GROUP)
    keep1, send1 = halves(1)
    arrived0, keep1, send1 = lax.optimization_barrier((arrived0, keep1, send1))

    def finish(keep, arrived):
        near = (keep[:outside] + arrived.astype(jnp.float32)).astype(jnp.bfloat16)
        return near, jnp.concatenate([near, keep[outside:].astype(jnp.bfloat16)], 0)

    arrived1 = shifted(send1, owners, GROUP)
    near0, fitted0 = finish(keep0, arrived0)
    ahead0 = shifted(near0, owners, -GROUP)
    near1, fitted1 = finish(keep1, arrived1)
    ahead0, near1, fitted1 = lax.optimization_barrier((ahead0, near1, fitted1))
    ahead1 = shifted(near1, owners, -GROUP)
    cut = slots // 2 // UNROLL * UNROLL
    ranges = [(0, cut), (cut, slots - cut)]
    before = contract(fitted0, ahead0, ranges, ())
    kept_a, sent_a = contract(fitted1, ahead1, ranges[:1], before[:2])
    swapped_a = swap(sent_a, bit=1)
    kept_b, sent_b = contract(fitted1, ahead1, ranges[1:], before[2:])
    swapped_a, kept_b, sent_b = lax.optimization_barrier((swapped_a, kept_b, sent_b))

    norm_factor = (aux_all * aux_parts * orbitals) ** (-0.5)
    both_a = kept_a + swapped_a.astype(jnp.float32)
    both_b = kept_b + swap(sent_b, bit=1).astype(jnp.float32)

    def through_pair(value):
        return value[0] + swap(value[1].astype(jnp.bfloat16), bit=2).astype(jnp.float32)

    if aux_parts == 2:
        rows = size // 2
        side = lax.axis_index("aux")

        def through_aux(value):
            dim = value.ndim - 2
            away = lax.dynamic_slice_in_dim(value, (1 - side) * rows, rows, dim)
            here = lax.dynamic_slice_in_dim(value, side * rows, rows, dim)
            other = lax.ppermute(away.astype(jnp.bfloat16), "aux", [(0, 1), (1, 0)])
            return here + other.astype(jnp.float32)

        early = through_aux(through_pair(both_a))
        late = through_pair(through_aux(both_b))
        summed = jnp.concatenate([early, late], 0)
    else:
        both = jnp.concatenate([both_a, both_b], 1)
        summed = lax.psum_scatter(through_pair(both), "aux", scatter_dimension=1, tiled=True)
    return (summed * norm_factor).astype(jnp.bfloat16)


def solution(mesh):
    in_specs = (P("ao", None), P("ao"), P("ao", "aux", None, None), P("ao", None))
    out_specs = P("ao", "aux", None)
    return jax.shard_map(
        on_device, mesh=mesh, in_specs=in_specs, out_specs=out_specs, check_vma=False
    )
```

```python
import functools

import jax
import jax.numpy as jnp
from jax import lax
from jax.experimental import pallas as pl
from jax.experimental.pallas import tpu as pltpu
from jax.sharding import PartitionSpec as P

GROUP = 4
REACH = 2
CHUNKS = 2
UNROLL = 4
VMEM_LIMIT = 48 * 1024 * 1024


def swapped(value, count, bit):
    return lax.ppermute(value, "ao", [(k, k ^ bit) for k in range(count)])


def shifted(value, count, steps):
    lo, hi = max(0, -steps), min(count, count - steps)
    return lax.ppermute(value, "ao", [(k, k + steps) for k in range(lo, hi)])


def halves_kernel(blocks, columns, info, pairs, *refs):
    tiles = refs[:GROUP]
    own, across, core_pair, ahead_a, ahead_b = refs[GROUP : GROUP + 5]
    keep_ref, send_ref = refs[GROUP + 5 : GROUP + 7]
    tile_v, coeff_v, totals, sems = refs[GROUP + 7 :]
    me = info[0]
    first = info[1]

    def place(source, start, index):
        return pltpu.make_async_copy(
            source.at[:, :, columns],
            coeff_v.at[pl.ds(start * blocks, blocks)],
            sems.at[index],
        )

    copies = [
        place(own, me, 0),
        place(across, me ^ 2, 1),
        place(core_pair.at[0], me ^ 1, 2),
        place(core_pair.at[1], me ^ 3, 3),
        place(ahead_a, GROUP + (me & 1), 4),
        place(ahead_b, GROUP + 1 - (me & 1), 5),
    ]
    copies += [
        pltpu.make_async_copy(tiles[d], tile_v.at[d], sems.at[6 + d]) for d in range(GROUP)
    ]
    for copy in copies:
        copy.start()
    totals[...] = jnp.zeros_like(totals)
    for copy in copies:
        copy.wait()

    aux_local = tile_v.shape[2]
    for d in range(GROUP):
        count = info[2 + d]

        def step(turn, carry):
            for aux in range(aux_local):
                updates = []
                for k in range(UNROLL):
                    slot = turn * UNROLL + k
                    left = pairs[d, 2 * slot] - first
                    right = pairs[d, 2 * slot + 1] - first
                    tile = tile_v[d, slot, aux]
                    tile = jnp.where(slot < count, tile, jnp.zeros_like(tile))
                    to_left = lax.dot_general(
                        tile, coeff_v[right], (((1,), (0,)), ((), ())),
                        preferred_element_type=jnp.float32,
                    )
                    to_right = lax.dot_general(
                        tile, coeff_v[left], (((0,), (0,)), ((), ())),
                        preferred_element_type=jnp.float32,
                    )
                    updates += [(left, to_left), (right, to_right)]
                for block, update in updates:
                    totals[block, aux] += update
            return carry

        lax.fori_loop(0, (count + UNROLL - 1) // UNROLL, step, 0)

    inside = GROUP * blocks
    keep_ref[...] = totals[:inside]
    send_ref[...] = totals[inside:].astype(send_ref.dtype)


def contract_kernel(blocks, ranges, earlier, info, pairs, *refs):
    own, ahead = refs[:2]
    before = refs[2:4] if earlier else None
    window, sems = refs[-2:]
    outs = refs[-2 - 2 * len(ranges) : -2]
    first = info[1]
    inside = GROUP * blocks
    copies = [
        pltpu.make_async_copy(own, window.at[pl.ds(0, inside)], sems.at[0]),
        pltpu.make_async_copy(ahead, window.at[pl.ds(inside, REACH * blocks)], sems.at[1]),
    ]
    for copy in copies:
        copy.start()
    for copy in copies:
        copy.wait()
    aux_local = window.shape[1]
    for r, (start, length) in enumerate(ranges):
        for d in range(GROUP):
            target = outs[2 * r + (d & 1)]
            base = before[d & 1] if earlier else None
            count = jnp.clip(info[2 + d] - start, 0, length)

            def step(turn, carry):
                results = []
                for k in range(UNROLL):
                    slot = turn * UNROLL + k
                    left = pairs[d, 2 * (start + slot)] - first
                    right = pairs[d, 2 * (start + slot) + 1] - first
                    total = base[d >> 1, slot] if earlier else None
                    for aux in range(aux_local):
                        part = lax.dot_general(
                            window[left, aux], window[right, aux], (((1,), (1,)), ((), ())),
                            preferred_element_type=jnp.float32,
                        )
                        total = part if total is None else total + part
                    total = jnp.where(slot < count, total, jnp.zeros_like(total))
                    results.append((slot, total))
                for slot, total in results:
                    target[d >> 1, slot] = total.astype(target.dtype)
                return carry

            def blank(turn, carry):
                for k in range(UNROLL):
                    target[d >> 1, turn * UNROLL + k] = jnp.zeros(target.shape[2:], target.dtype)
                return carry

            turns = (count + UNROLL - 1) // UNROLL
            lax.fori_loop(0, turns, step, 0)
            lax.fori_loop(turns, length // UNROLL, blank, 0)


def on_device(pair_list, pair_count, tiles, coeff):
    slots, aux_all, size, _ = tiles.shape
    orbitals = coeff.shape[1]
    blocks = coeff.shape[0] // size
    owners = lax.axis_size("ao")
    aux_parts = lax.axis_size("aux")
    aux_local = aux_all // GROUP
    owner = lax.axis_index("ao")
    me = owner % GROUP
    first = (owner - me) * blocks
    swap = functools.partial(swapped, count=owners)

    def part_of(member):
        return lax.dynamic_slice_in_dim(tiles, member * aux_local, aux_local, 1)

    own = coeff.reshape(blocks, size, orbitals)
    listed = jnp.concatenate([pair_list.reshape(-1), pair_count]).reshape(1, -1)
    lists = jnp.concatenate([listed] + [swap(listed, bit=d) for d in range(1, GROUP)], 0)
    parts = [part_of(me ^ d) for d in range(GROUP)]
    across, lists, parts = lax.optimization_barrier((swap(own, bit=2), lists, parts))
    handed_on = swap(swap(parts[3], bit=2), bit=1)
    group_tiles = [parts[0], swap(parts[1], bit=1), swap(parts[2], bit=2), handed_on]
    core_pair = swap(jnp.stack([own, across]), bit=1)
    ahead_a = shifted(jnp.where(me < REACH, own, across), owners, -GROUP)
    ahead_b = swap(ahead_a, bit=1)

    counts = lists[:, 2 * slots]
    info = jnp.concatenate([jnp.stack([me, first]).astype(jnp.int32), counts])

    smem = pl.BlockSpec(memory_space=pltpu.SMEM)
    anywhere = pl.BlockSpec(memory_space=pl.ANY)
    vmem = pl.BlockSpec(memory_space=pltpu.VMEM)
    inside, outside = GROUP * blocks, REACH * blocks
    window = inside + outside
    width = orbitals // CHUNKS

    def halves(chunk):
        columns = slice(chunk * width, (chunk + 1) * width)
        return pl.pallas_call(
            functools.partial(halves_kernel, blocks, columns),
            out_shape=(
                jax.ShapeDtypeStruct((inside, aux_local, size, width), jnp.float32),
                jax.ShapeDtypeStruct((outside, aux_local, size, width), jnp.bfloat16),
            ),
            in_specs=[smem] * 2 + [anywhere] * (GROUP + 5),
            out_specs=(vmem, vmem),
            scratch_shapes=[
                pltpu.VMEM((GROUP, slots, aux_local, size, size), jnp.bfloat16),
                pltpu.VMEM((window, size, width), jnp.bfloat16),
                pltpu.VMEM((window, aux_local, size, width), jnp.float32),
                pltpu.SemaphoreType.DMA((6 + GROUP,)),
            ],
            compiler_params=pltpu.CompilerParams(vmem_limit_bytes=VMEM_LIMIT),
            cost_estimate=pl.CostEstimate(
                flops=8 * GROUP * slots * aux_local * size * size * width,
                bytes_accessed=32 * 1024 * 1024,
                transcendentals=0,
            ),
            name="halves",
        )(info, lists, *group_tiles, own, across, core_pair, ahead_a, ahead_b)

    def contract(fitted, fitted_ahead, ranges, before):
        last = len(before) > 0
        shapes = []
        for _, length in ranges:
            shape = (2, length, size, size)
            shapes.append(jax.ShapeDtypeStruct(shape, jnp.float32))
            shapes.append(jax.ShapeDtypeStruct(shape, jnp.bfloat16 if last else jnp.float32))
        return pl.pallas_call(
            functools.partial(contract_kernel, blocks, ranges, last),
            out_shape=tuple(shapes),
            in_specs=[smem] * 2 + [anywhere] * 2 + [vmem] * len(before),
            out_specs=(vmem,) * len(shapes),
            scratch_shapes=[
                pltpu.VMEM((window, aux_local, size, width), jnp.bfloat16),
                pltpu.SemaphoreType.DMA((2,)),
            ],
            compiler_params=pltpu.CompilerParams(vmem_limit_bytes=VMEM_LIMIT),
            cost_estimate=pl.CostEstimate(
                flops=4 * GROUP * slots * aux_local * size * size * width,
                bytes_accessed=16 * 1024 * 1024,
                transcendentals=0,
            ),
            name="contract",
        )(info, lists, fitted, fitted_ahead, *before)

    keep0, send0 = halves(0)
    arrived0 = shifted(send0, owners, GROUP)
    keep1, send1 = halves(1)
    arrived0, keep1, send1 = lax.optimization_barrier((arrived0, keep1, send1))

    def finish(keep, arrived):
        near = (keep[:outside] + arrived.astype(jnp.float32)).astype(jnp.bfloat16)
        return near, jnp.concatenate([near, keep[outside:].astype(jnp.bfloat16)], 0)

    arrived1 = shifted(send1, owners, GROUP)
    near0, fitted0 = finish(keep0, arrived0)
    ahead0 = shifted(near0, owners, -GROUP)
    near1, fitted1 = finish(keep1, arrived1)
    ahead0, near1, fitted1 = lax.optimization_barrier((ahead0, near1, fitted1))
    ahead1 = shifted(near1, owners, -GROUP)
    cut = slots // 2 // UNROLL * UNROLL
    ranges = [(0, cut), (cut, slots - cut)]
    before = contract(fitted0, ahead0, ranges, ())
    kept_a, sent_a = contract(fitted1, ahead1, ranges[:1], before[:2])
    swapped_a = swap(sent_a, bit=1)
    kept_b, sent_b = contract(fitted1, ahead1, ranges[1:], before[2:])
    swapped_a, kept_b, sent_b = lax.optimization_barrier((swapped_a, kept_b, sent_b))

    norm_factor = (aux_all * aux_parts * orbitals) ** (-0.5)
    both_a = kept_a + swapped_a.astype(jnp.float32)
    both_b = kept_b + swap(sent_b, bit=1).astype(jnp.float32)

    def through_pair(value):
        return value[0] + swap(value[1].astype(jnp.bfloat16), bit=2).astype(jnp.float32)

    if aux_parts == 2:
        rows = size // 2
        side = lax.axis_index("aux")

        def through_aux(value):
            dim = value.ndim - 2
            away = lax.dynamic_slice_in_dim(value, (1 - side) * rows, rows, dim)
            here = lax.dynamic_slice_in_dim(value, side * rows, rows, dim)
            other = lax.ppermute(away.astype(jnp.bfloat16), "aux", [(0, 1), (1, 0)])
            return here + other.astype(jnp.float32)

        early = through_aux(through_pair(both_a))
        late = through_pair(through_aux(both_b))
        summed = jnp.concatenate([early, late], 0)
    else:
        both = jnp.concatenate([both_a, both_b], 1)
        summed = lax.psum_scatter(through_pair(both), "aux", scatter_dimension=1, tiled=True)
    return (summed * norm_factor).astype(jnp.bfloat16)


def solution(mesh):
    in_specs = (P("ao", None), P("ao"), P("ao", "aux", None, None), P("ao", None))
    out_specs = P("ao", "aux", None)
    return jax.shard_map(
        on_device, mesh=mesh, in_specs=in_specs, out_specs=out_specs, check_vma=False
    )
```
